32 devices in a mesh: rep: 2 (over x), shard: 4 (over y, core), head: 4 (over z).
Axes of the slice: x: 2, y: 2, z: 4, core: 2. Of those that a mesh axis runs over, the one named last changes fastest.
Arguments:
- tokens: bfloat16 [8192, 1024], P(('rep', 'shard', 'head')), may hold values from -6 to 6
- ln1_gain: bfloat16 [1024], P('shard'), may hold values from 0.25 to 1.75
- ln1_bias: bfloat16 [1024], P('shard'), may hold values from -3 to 3
- w_query: bfloat16 [1024, 1024], P('shard', 'head'), may hold values from -0.1875 to 0.1875
- w_key: bfloat16 [1024, 1024], P('shard', 'head'), may hold values from -0.1875 to 0.1875
- w_value: bfloat16 [1024, 1024], P('shard', 'head'), may hold values from -0.1875 to 0.1875
- b_query: bfloat16 [16, 64], P('head', 'shard'), may hold values from -4 to 4
- b_value: bfloat16 [16, 64], P('head', 'shard'), may hold values from -4 to 4
- w_out: bfloat16 [1024, 1024], P('head', 'shard'), may hold values from -0.75 to 0.75
- b_out: bfloat16 [1024], P('shard'), may hold values from -3 to 3
- ln2_gain: bfloat16 [1024], P('shard'), may hold values from 0.25 to 1.75
- ln2_bias: bfloat16 [1024], P('shard'), may hold values from -3 to 3
- w_up: bfloat16 [1024, 4096], P('shard', 'head'), may hold values from -0.1875 to 0.1875
- b_up: bfloat16 [32, 128], P('head', 'shard'), may hold values from -4 to 4
- w_down: bfloat16 [4096, 1024], P('head', 'shard'), may hold values from -0.125 to 0.125
- b_down: bfloat16 [1024], P('shard'), may hold values from -3 to 3
- cotangent: bfloat16 [8192, 1024], P(('rep', 'shard', 'head')), may hold values from -6 to 6
Outputs:
- output: bfloat16 [8192, 1024], P(('rep', 'shard', 'head'))
- input_grad: bfloat16 [8192, 1024], P(('rep', 'shard', 'head'))
- ln1_gain_grad: float32 [1024], P('shard')
- ln1_bias_grad: float32 [1024], P('shard')
- w_query_grad: float32 [1024, 1024], P('shard', 'head')
- w_key_grad: float32 [1024, 1024], P('shard', 'head')
- w_value_grad: float32 [1024, 1024], P('shard', 'head')
- b_query_grad: float32 [16, 64], P('head', 'shard')
- b_value_grad: float32 [16, 64], P('head', 'shard')
- w_out_grad: float32 [1024, 1024], P('head', 'shard')
- b_out_grad: float32 [1024], P('shard')
- ln2_gain_grad: float32 [1024], P('shard')
- ln2_bias_grad: float32 [1024], P('shard')
- w_up_grad: float32 [1024, 4096], P('shard', 'head')
- b_up_grad: float32 [32, 128], P('head', 'shard')
- w_down_grad: float32 [4096, 1024], P('head', 'shard')
- b_down_grad: float32 [1024], P('shard')
The draws below stay inside these ranges and needn't reach their ends.
All inputs are finite; a program needn't handle non-finite values.
Results may differ from the reference program's by a relative error of at most 0.02.
Values may be sent and summed in bfloat16 or wider, within the bound.
A program may use at most 128 MiB of HBM per device.

```python
import jax
import jax.numpy as jnp
from jax import lax

D = 1024
HEADS = 16
HD = 64
FF = 4096
SEQ = 1024
TOKENS = 8192


def block_levels(stream_key, shape, cuts, least, largest):
    factor_of, own = 1.0, jax.random.fold_in(stream_key, 6)
    for axis_at, parts in cuts:
        steps = jnp.exp(jax.random.uniform(jax.random.fold_in(own, axis_at), (parts,), jnp.float32, least / len(cuts), largest / len(cuts)))
        factor_of = factor_of * jnp.repeat(steps, shape[axis_at] // parts).reshape([-1 if axis == axis_at else 1 for axis in range(len(shape))])
    return factor_of


def gaussian(own_key, shape, width, most, pieces=(), kind=jnp.bfloat16):
    drawn = jax.random.normal(own_key, shape, jnp.float32) * width
    if len(pieces) > 0:
        drawn = block_levels(own_key, shape, pieces, -0.22, 0.18) * drawn
    return jnp.clip(drawn, min=-most, max=most).astype(kind)


def setup_inputs(seed: int = 0) -> dict:
    streams_of = jax.random.split(jax.random.key(seed), 18)
    return {
        "tokens": gaussian(streams_of[0], (TOKENS, D), 1.0, 6.0, ((0, 32),)),
        "ln1_gain": jnp.clip(1.0 + 0.15 * jax.random.normal(streams_of[1], (D,), jnp.float32), 0.25, 1.75).astype(jnp.bfloat16),
        "ln1_bias": gaussian(streams_of[2], (D,), 0.3, 3.0, ((0, 4),)),
        "w_query": gaussian(streams_of[3], (D, D), D ** -0.5, 0.1875, ((0, 4), (1, 4))),
        "w_key": gaussian(streams_of[4], (D, D), D ** -0.5, 0.1875, ((0, 4), (1, 4))),
        "w_value": gaussian(streams_of[5], (D, D), D ** -0.5, 0.1875, ((0, 4), (1, 4))),
        "b_query": gaussian(streams_of[6], (HEADS, HD), 0.5, 4.0, ((0, 4), (1, 4))),
        "b_value": gaussian(streams_of[7], (HEADS, HD), 0.5, 4.0, ((0, 4), (1, 4))),
        "w_out": gaussian(streams_of[8], (D, D), (D // 16) ** -0.5, 0.75, ((0, 4), (1, 4))),
        "b_out": gaussian(streams_of[9], (D,), 0.3, 3.0, ((0, 4),)),
        "ln2_gain": jnp.clip(1.0 + 0.15 * jax.random.normal(streams_of[10], (D,), jnp.float32), 0.25, 1.75).astype(jnp.bfloat16),
        "ln2_bias": gaussian(streams_of[11], (D,), 0.3, 3.0, ((0, 4),)),
        "w_up": gaussian(streams_of[12], (D, FF), D ** -0.5, 0.1875, ((0, 4), (1, 4))),
        "b_up": gaussian(streams_of[13], (FF // 128, 128), 0.5, 4.0, ((0, 4), (1, 4))),
        "w_down": gaussian(streams_of[14], (FF, D), (FF // 2) ** -0.5, 0.125, ((0, 4), (1, 4))),
        "b_down": gaussian(streams_of[15], (D,), 0.3, 3.0, ((0, 4),)),
        "cotangent": gaussian(streams_of[16], (TOKENS, D), 1.0, 6.0, ((0, 32),)),
    }


@jax.custom_vjp
def low(v):
    return lax.optimization_barrier(v.astype(jnp.bfloat16)).astype(jnp.float32)

@jax.custom_vjp
def low_back(v):
    return v

def low_keep(v):
    return (low(v), None)

def low_pass(kept, grad):
    return (grad,)

def back_keep(v):
    return (v, None)

def back_low(kept, grad):
    return (low(grad),)
low.defvjp(low_keep, low_pass)
low_back.defvjp(back_keep, back_low)
highest = lax.Precision.HIGHEST

def matmul(left, right):
    return jnp.dot(left, right, precision=highest, preferred_element_type=jnp.float32)

def normalize(rows, gain, bias):
    mean = lax.optimization_barrier(jnp.mean(rows, axis=-1, keepdims=True))
    centred = rows - mean
    spread = lax.optimization_barrier(jnp.mean(centred * centred, axis=-1, keepdims=True))
    return centred * lax.rsqrt(spread + 1e-05) * gain + bias

def attend_block(queries, keys, values, start, slopes, block):
    scores = jnp.einsum('qhd,khd->hqk', queries, keys, precision=highest) * HD ** (-0.5)
    later = start + jnp.arange(block, dtype=jnp.int32)
    earlier = jnp.arange(SEQ, dtype=jnp.int32)
    distance = (later[:, None] - earlier[None, :]).astype(jnp.float32)
    scores = low_back(scores - slopes[:, None, None] * distance)
    scores = jnp.where(distance >= 0, scores, -1e+30)
    probs = low(jax.nn.softmax(scores, axis=-1))
    mixed = jnp.einsum('hqk,khd->qhd', probs, values, precision=highest)
    return low_back(low(mixed))

def attention(queries, keys, values):
    block = min(512, SEQ)
    count = SEQ // block
    slopes = jnp.exp2(-8.0 * (jnp.arange(HEADS, dtype=jnp.int32) + 1).astype(jnp.float32) / HEADS)
    query_blocks = queries.reshape(count, block, HEADS, HD)
    key_heads = keys.reshape(SEQ, HEADS, HD)
    value_heads = values.reshape(SEQ, HEADS, HD)
    starts = jnp.arange(count, dtype=jnp.int32) * block
    checked = jax.checkpoint(lambda chosen, start: attend_block(chosen, key_heads, value_heads, start, slopes, block))
    mixed = lax.map(lambda pair: checked(pair[0], pair[1]), (query_blocks, starts))
    return mixed.reshape(SEQ, D)

def layer(rows, ln1_gain, ln1_bias, w_query, w_key, w_value, b_query, b_value, w_out, b_out, ln2_gain, ln2_bias, w_up, b_up, w_down, b_down):
    normed_one = low(normalize(rows, ln1_gain, ln1_bias))
    queries = low_back(low(matmul(normed_one, w_query) + b_query.reshape(-1)))
    keys = low_back(low(matmul(normed_one, w_key)))
    values = low_back(low(matmul(normed_one, w_value) + b_value.reshape(-1)))
    mixed = attention(queries, keys, values)
    branch = low_back(matmul(mixed, w_out))
    resid = rows + branch + b_out
    normed_two = low(normalize(resid, ln2_gain, ln2_bias))
    hidden_pre = low_back(matmul(normed_two, w_up) + b_up.reshape(-1))
    hidden = low(jax.nn.gelu(hidden_pre, approximate=True))
    feed = low_back(matmul(hidden, w_down))
    return resid + feed + b_down

def reference(tokens, ln1_gain, ln1_bias, w_query, w_key, w_value, b_query, b_value, w_out, b_out, ln2_gain, ln2_bias, w_up, b_up, w_down, b_down, cotangent):
    params = tuple((item.astype(jnp.float32) for item in (ln1_gain, ln1_bias, w_query, w_key, w_value, b_query, b_value, w_out, b_out, ln2_gain, ln2_bias, w_up, b_up, w_down, b_down)))
    rows = tokens.astype(jnp.float32).reshape(-1, SEQ, D)
    upstream = cotangent.astype(jnp.float32).reshape(-1, SEQ, D)

    def step(totals, pair):
        seq_rows, seq_grad = pair
        result, backward = jax.vjp(layer, seq_rows, *params)
        grads = backward(seq_grad)
        totals = tuple((total + grad for total, grad in zip(totals, grads[1:])))
        return (totals, (result, grads[0]))
    zeros = tuple((jnp.zeros_like(item) for item in params))
    totals, (outputs, input_grads) = lax.scan(step, zeros, (rows, upstream))
    return (outputs.reshape(-1, D).astype(jnp.bfloat16), input_grads.reshape(-1, D).astype(jnp.bfloat16), totals[0], totals[1], totals[2], totals[3], totals[4], totals[5], totals[6], totals[7], totals[8], totals[9], totals[10], totals[11], totals[12], totals[13], totals[14])
```

```python
from functools import partial

import jax
import jax.numpy as jnp
from jax import lax
from jax.experimental import pallas as pl
from jax.experimental.pallas import tpu as pltpu
from jax.sharding import PartitionSpec as P

HEADS = 16
HD = 64
SEQ = 1024
BF = jnp.bfloat16
F32 = jnp.float32


def contract(left, right, left_dim, right_dim):
    return lax.dot_general(
        left, right, (((left_dim,), (right_dim,)), ((), ())), preferred_element_type=F32
    )


def layer_norm(rows, gain, bias):
    mean = jnp.mean(rows, axis=-1, keepdims=True)
    centred = rows - mean
    spread = jnp.mean(centred * centred, axis=-1, keepdims=True)
    return centred * lax.rsqrt(spread + 1e-05) * gain + bias


def swap(value, axis, bit):
    size = lax.axis_size(axis)
    return lax.ppermute(value, axis, [(at, at ^ bit) for at in range(size)])


def spread_blocks(own):
    beside = swap(own, "shard", 1)
    across = swap(own, "shard", 2)
    corner = swap(across, "shard", 1)
    return jnp.concatenate([own, across, beside, corner], axis=0)


def blocks_by_xor(value, shard, axis):
    width = value.shape[axis] // 4
    low_bit = lax.rem(shard, 2) == 1
    high_bit = shard >= 2
    parts = [lax.slice_in_dim(value, at * width, (at + 1) * width, axis=axis) for at in range(4)]
    a, b, c, d = parts
    a, b, c, d = (
        jnp.where(low_bit, b, a), jnp.where(low_bit, a, b),
        jnp.where(low_bit, d, c), jnp.where(low_bit, c, d),
    )
    a, b, c, d = (
        jnp.where(high_bit, c, a), jnp.where(high_bit, d, b),
        jnp.where(high_bit, a, c), jnp.where(high_bit, b, d),
    )
    return jnp.concatenate([a, c, b, d], axis=axis)


def blocks_back(value, shard, axis):
    width = value.shape[axis] // 4
    a, c, b, d = [
        lax.slice_in_dim(value, at * width, (at + 1) * width, axis=axis) for at in range(4)
    ]
    low_bit = lax.rem(shard, 2) == 1
    high_bit = shard >= 2
    a, b, c, d = (
        jnp.where(high_bit, c, a), jnp.where(high_bit, d, b),
        jnp.where(high_bit, a, c), jnp.where(high_bit, b, d),
    )
    a, b, c, d = (
        jnp.where(low_bit, b, a), jnp.where(low_bit, a, b),
        jnp.where(low_bit, d, c), jnp.where(low_bit, c, d),
    )
    return jnp.concatenate([a, b, c, d], axis=axis)


def gather_rows(own):
    size = lax.axis_size("head")
    pieces = [own]
    for step in range(1, size):
        pieces.append(lax.ppermute(own, "head", [(at, (at - step) % size) for at in range(size)]))
    return jnp.concatenate(pieces, axis=0)


def scatter_rows(total):
    size = lax.axis_size("head")
    rows = total.shape[0] // size
    out = total[:rows].astype(F32)
    for step in range(1, size):
        piece = total[step * rows : (step + 1) * rows]
        out = out + lax.ppermute(
            piece, "head", [(at, (at + step) % size) for at in range(size)]
        ).astype(F32)
    return out


def scatter_grad(grad):
    width = grad.shape[0] // 4
    near = (
        grad[: 2 * width] + swap(grad[2 * width :].astype(BF), "shard", 1).astype(F32)
    )
    own = near[:width] + swap(near[width:].astype(BF), "shard", 2).astype(F32)
    own = own.astype(BF)
    if lax.axis_size("rep") == 2:
        return own.astype(F32) + swap(own, "rep", 1).astype(F32)
    return lax.psum(own.astype(F32), "rep")


def forward_kernel(count, block, slopes, starts, q_ref, k_ref, v_ref, o_ref, lse_ref):
    pair = pl.program_id(0)
    key_at = lax.broadcasted_iota(jnp.int32, (block, block), 0)
    query_at = lax.broadcasted_iota(jnp.int32, (block, block), 1)
    gap = (query_at - key_at).astype(F32)
    seen = query_at >= key_at
    rows = [pl.ds(pl.multiple_of(starts[at], block), block) for at in range(count)]
    for head in range(2):
        lanes = pl.ds(head * HD, HD)
        slope = slopes[pair * 2 + head]
        tilt = gap * slope
        for at in range(count):
            query = q_ref[rows[at], lanes]
            tiles = []
            for to in range(at + 1):
                tile = contract(k_ref[rows[to], lanes], query, 1, 1)
                tile = tile - (tilt + slope * float((at - to) * block))
                if to == at:
                    tile = jnp.where(seen, tile, -1e30)
                tiles.append(tile)
            top = jnp.max(tiles[0], axis=0, keepdims=True)
            for tile in tiles[1:]:
                top = jnp.maximum(top, jnp.max(tile, axis=0, keepdims=True))
            tiles = [jnp.exp(tile - top) for tile in tiles]
            total = jnp.sum(tiles[0], axis=0, keepdims=True)
            for tile in tiles[1:]:
                total = total + jnp.sum(tile, axis=0, keepdims=True)
            share = 1.0 / total
            mixed = None
            for to in range(at + 1):
                piece = contract(v_ref[rows[to], lanes], (tiles[to] * share).astype(BF), 0, 0)
                mixed = piece if mixed is None else mixed + piece
            o_ref[rows[at], lanes] = mixed.T.astype(BF)
            lse_ref[0, pl.ds(head * count + at, 1), :] = top + jnp.log(total)


def backward_kernel(
    count, block, slopes, starts, q_ref, k_ref, v_ref, g_ref, lse_ref,
    dq_ref, dk_ref, dv_ref, dk_sum, dv_sum,
):
    pair = pl.program_id(0)
    key_at = lax.broadcasted_iota(jnp.int32, (block, block), 0)
    query_at = lax.broadcasted_iota(jnp.int32, (block, block), 1)
    gap = (query_at - key_at).astype(F32)
    seen = query_at >= key_at
    rows = [pl.ds(pl.multiple_of(starts[at], block), block) for at in range(count)]
    for head in range(2):
        lanes = pl.ds(head * HD, HD)
        slope = slopes[pair * 2 + head]
        tilt = gap * slope
        for at in reversed(range(count)):
            query = q_ref[rows[at], lanes]
            grad = g_ref[rows[at], lanes]
            lse = lse_ref[0, pl.ds(head * count + at, 1), :]
            probs, grads = [], []
            inner = None
            for to in range(at + 1):
                tile = contract(k_ref[rows[to], lanes], query, 1, 1)
                tile = tile - (tilt + (slope * float((at - to) * block) + lse))
                if to == at:
                    tile = jnp.where(seen, tile, -1e30)
                prob = jnp.exp(tile)
                prob_grad = contract(v_ref[rows[to], lanes], grad, 1, 1)
                part = jnp.sum(prob * prob_grad, axis=0, keepdims=True)
                inner = part if inner is None else inner + part
                probs.append(prob)
                grads.append(prob_grad)
            query_grad = None
            for to in range(at + 1):
                score_grad = (probs[to] * (grads[to] - inner)).astype(BF)
                piece = contract(k_ref[rows[to], lanes], score_grad, 0, 0)
                query_grad = piece if query_grad is None else query_grad + piece
                key_piece = contract(score_grad, query, 1, 0)
                value_piece = contract(probs[to].astype(BF), grad, 1, 0)
                span = pl.ds(to * block, block)
                if at == count - 1:
                    dk_sum[span, :] = key_piece
                    dv_sum[span, :] = value_piece
                else:
                    dk_sum[span, :] += key_piece
                    dv_sum[span, :] += value_piece
            dq_ref[rows[at], lanes] = (query_grad.T * HD**-0.5).astype(BF)
        for to in range(count):
            span = pl.ds(to * block, block)
            dk_ref[rows[to], lanes] = dk_sum[span, :].astype(BF)
            dv_ref[rows[to], lanes] = dv_sum[span, :].astype(BF)


def attend(qkv, slopes, starts, block):
    seq, width = qkv.shape[0], qkv.shape[1] // 3
    pairs, count = width // 128, seq // block

    def at(first):
        return pl.BlockSpec((seq, 128), lambda pair: (0, first * pairs + pair))

    scalar = pl.BlockSpec(memory_space=pltpu.SMEM)
    return pl.pallas_call(
        partial(forward_kernel, count, block),
        grid=(pairs,),
        in_specs=[scalar, scalar, at(0), at(1), at(2)],
        out_specs=[at(0), pl.BlockSpec((1, 2 * count, block), lambda pair: (pair, 0, 0))],
        out_shape=[
            jax.ShapeDtypeStruct((seq, width), BF),
            jax.ShapeDtypeStruct((pairs, 2 * count, block), F32),
        ],
        compiler_params=pltpu.CompilerParams(vmem_limit_bytes=32 * 2**20),
        name="attend",
    )(slopes, starts, qkv, qkv, qkv)


def attend_back(qkv, grad, logsum, slopes, starts, block):
    seq, width = grad.shape
    pairs, count = width // 128, seq // block

    def at(first):
        return pl.BlockSpec((seq, 128), lambda pair: (0, first * pairs + pair))

    scalar = pl.BlockSpec(memory_space=pltpu.SMEM)
    shape = jax.ShapeDtypeStruct((seq, width), BF)
    return pl.pallas_call(
        partial(backward_kernel, count, block),
        grid=(pairs,),
        in_specs=[
            scalar, scalar, at(0), at(1), at(2), at(0),
            pl.BlockSpec((1, 2 * count, block), lambda pair: (pair, 0, 0)),
        ],
        out_specs=[at(0), at(0), at(0)],
        out_shape=[shape, shape, shape],
        scratch_shapes=[pltpu.VMEM((seq, HD), F32), pltpu.VMEM((seq, HD), F32)],
        compiler_params=pltpu.CompilerParams(vmem_limit_bytes=32 * 2**20),
        name="attend_back",
    )(slopes, starts, qkv, qkv, qkv, grad, logsum)


def body(
    tokens,
    ln1_gain,
    ln1_bias,
    w_query,
    w_key,
    w_value,
    b_query,
    b_value,
    w_out,
    b_out,
    ln2_gain,
    ln2_bias,
    w_up,
    b_up,
    w_down,
    b_down,
    cotangent,
):
    shard = lax.axis_index("shard")
    place = lax.axis_index("head")
    group = lax.axis_size("head")
    heads_here = b_query.shape[0]
    width = w_query.shape[1]
    ffn = w_up.shape[1]
    feats = ln1_gain.shape[0]
    block = tokens.shape[0]

    attn_w = spread_blocks(jnp.concatenate([w_query, w_key, w_value, w_out.T], axis=1))
    small = jnp.concatenate(
        [ln1_gain, ln1_bias, b_out, ln2_gain, ln2_bias, b_down]
        + [b_query.reshape(-1), b_value.reshape(-1), b_up.reshape(-1)]
    )
    small = lax.all_gather(small, "shard", axis=0)
    rows6 = small[:, : 6 * feats].reshape(4, 6, feats)
    rows6 = rows6.transpose(1, 0, 2).reshape(6, 4 * feats).astype(F32)
    gain_one, shift_one, out_b, gain_two, shift_two, down_b = blocks_by_xor(rows6, shard, 1)
    at = 6 * feats
    step = b_query.size
    query_b = small[:, at : at + step].reshape(4, heads_here, -1).transpose(1, 0, 2).reshape(-1)
    at += step
    value_b = small[:, at : at + step].reshape(4, heads_here, -1).transpose(1, 0, 2).reshape(-1)
    at += step
    up_b = small[:, at:].reshape(4, b_up.shape[0], -1).transpose(1, 0, 2).reshape(-1).astype(F32)
    qkv_b = jnp.concatenate([query_b, jnp.zeros_like(query_b), value_b]).astype(F32)

    inputs = blocks_by_xor(tokens, shard, 1).astype(F32)
    cot = blocks_by_xor(cotangent, shard, 1)
    normed_one = gather_rows(layer_norm(inputs, gain_one, shift_one).astype(BF))
    up_w = spread_blocks(w_up)
    down_w = spread_blocks(w_down.T)
    mlp_grad = gather_rows(cot)

    qkv_w = attn_w[:, : 3 * width]
    out_w = attn_w[:, 3 * width :]
    factor = jnp.concatenate([jnp.full((width,), HD**-0.5, F32), jnp.ones((2 * width,), F32)])
    qkv = ((jnp.dot(normed_one, qkv_w, preferred_element_type=F32) + qkv_b) * factor).astype(BF)
    position = place * heads_here + jnp.arange(heads_here, dtype=jnp.int32) + 1
    slopes = jnp.exp2(-8.0 * position.astype(F32) / HEADS)
    starts = lax.rem(jnp.arange(group, dtype=jnp.int32) - place + group, group) * block
    mixed, logsum = attend(qkv, slopes, starts, block)
    resid = inputs + scatter_rows(contract(mixed, out_w, 1, 1).astype(BF)) + out_b
    normed_two = gather_rows(layer_norm(resid, gain_two, shift_two).astype(BF))
    hidden_pre = jnp.dot(normed_two, up_w, preferred_element_type=F32) + up_b
    hidden = jax.nn.gelu(hidden_pre, approximate=True).astype(BF)
    hidden_grad = jnp.dot(mlp_grad, down_w, preferred_element_type=F32)
    unused, gelu_back = jax.vjp(partial(jax.nn.gelu, approximate=True), hidden_pre)
    pre_grad_f = gelu_back(hidden_grad)[0]
    pre_grad = pre_grad_f.astype(BF)
    second_grad = scatter_rows(contract(pre_grad, up_w, 1, 1).astype(BF))
    output = resid + scatter_rows(contract(hidden, down_w, 1, 1).astype(BF)) + down_b
    output = blocks_back(output.astype(BF), shard, 1)
    upstream = cot.astype(F32)
    down_b_grad = jnp.sum(upstream, axis=0)
    down_w_grad = scatter_grad(contract(mlp_grad, hidden, 0, 0))
    up_w_grad = scatter_grad(contract(normed_two, pre_grad, 0, 0))
    up_b_grad = jnp.sum(pre_grad.astype(F32), axis=0)
    unused, norm_back = jax.vjp(layer_norm, resid, gain_two, shift_two)
    resid_part, gain_two_grad, shift_two_grad = norm_back(second_grad)
    resid_grad = upstream + resid_part
    out_b_grad = jnp.sum(resid_grad, axis=0)
    attn_grad = gather_rows(resid_grad.astype(BF))
    mixed_grad = jnp.dot(attn_grad, out_w, preferred_element_type=F32).astype(BF)
    out_w_grad = scatter_grad(contract(attn_grad, mixed, 0, 0))
    query_grad, key_grad, value_grad = attend_back(qkv, mixed_grad, logsum, slopes, starts, block)
    qkv_grad = jnp.concatenate([query_grad, key_grad, value_grad], axis=1)
    first_grad = scatter_rows(contract(qkv_grad, qkv_w, 1, 1).astype(BF))
    qkv_w_grad = scatter_grad(contract(normed_one, qkv_grad, 0, 0))
    query_b_grad = jnp.sum(query_grad.astype(F32), axis=0)
    value_b_grad = jnp.sum(value_grad.astype(F32), axis=0)
    unused, first_back = jax.vjp(layer_norm, inputs, gain_one, shift_one)
    input_part, gain_one_grad, shift_one_grad = first_back(first_grad)
    input_grad = blocks_back((resid_grad + input_part).astype(BF), shard, 1)

    stats = jnp.stack(
        [gain_one_grad, shift_one_grad, out_b_grad, gain_two_grad, shift_two_grad, down_b_grad]
    )
    stats = blocks_back(stats, shard, 1).reshape(-1)
    biases = jnp.concatenate([query_b_grad, value_b_grad, up_b_grad])
    mine = (jnp.arange(group, dtype=jnp.int32) == place)[:, None]
    biases = jnp.where(mine, biases[None, :], 0.0).reshape(-1)
    sums = lax.psum(jnp.concatenate([stats, biases]), ("rep", "shard", "head"))
    stats = sums[: stats.size].reshape(6, 4, feats)
    stats = lax.dynamic_index_in_dim(stats, shard, 1, keepdims=False)
    biases = lax.dynamic_index_in_dim(
        sums[6 * 4 * feats :].reshape(group, -1), place, 0, keepdims=False
    )

    def own_part(values, rows):
        parts = values.reshape(rows, 4, -1)
        return lax.dynamic_index_in_dim(parts, shard, 1, keepdims=False)

    return (
        output,
        input_grad,
        stats[0],
        stats[1],
        qkv_w_grad[:, :width],
        qkv_w_grad[:, width : 2 * width],
        qkv_w_grad[:, 2 * width :],
        own_part(biases[:width], heads_here),
        own_part(biases[width : 2 * width], heads_here),
        out_w_grad.T,
        stats[2],
        stats[3],
        stats[4],
        up_w_grad,
        own_part(biases[2 * width :], b_up.shape[0]),
        down_w_grad.T,
        stats[5],
    )


def solution(mesh):
    return jax.shard_map(
        body,
        mesh=mesh,
        in_specs=(
            P(("rep", "shard", "head"), None),
            P("shard"),
            P("shard"),
            P("shard", "head"),
            P("shard", "head"),
            P("shard", "head"),
            P("head", "shard"),
            P("head", "shard"),
            P("head", "shard"),
            P("shard"),
            P("shard"),
            P("shard"),
            P("shard", "head"),
            P("head", "shard"),
            P("head", "shard"),
            P("shard"),
            P(("rep", "shard", "head"), None),
        ),
        out_specs=(
            P(("rep", "shard", "head"), None),
            P(("rep", "shard", "head"), None),
            P("shard"),
            P("shard"),
            P("shard", "head"),
            P("shard", "head"),
            P("shard", "head"),
            P("head", "shard"),
            P("head", "shard"),
            P("head", "shard"),
            P("shard"),
            P("shard"),
            P("shard"),
            P("shard", "head"),
            P("head", "shard"),
            P("head", "shard"),
            P("shard"),
        ),
        check_vma=False,
    )
```

```python
from functools import partial

import jax
import jax.numpy as jnp
from jax import lax
from jax.experimental import pallas as pl
from jax.experimental.pallas import tpu as pltpu
from jax.sharding import PartitionSpec as P

HEADS = 16
HD = 64
SEQ = 1024
BF = jnp.bfloat16
F32 = jnp.float32


def contract(left, right, left_dim, right_dim):
    return lax.dot_general(
        left, right, (((left_dim,), (right_dim,)), ((), ())), preferred_element_type=F32
    )


def layer_norm(rows, gain, bias):
    mean = jnp.mean(rows, axis=-1, keepdims=True)
    centred = rows - mean
    spread = jnp.mean(centred * centred, axis=-1, keepdims=True)
    return centred * lax.rsqrt(spread + 1e-05) * gain + bias


def swap(value, axis, bit):
    size = lax.axis_size(axis)
    return lax.ppermute(value, axis, [(at, at ^ bit) for at in range(size)])


def spread_blocks(own):
    beside = swap(own, "shard", 1)
    across = swap(own, "shard", 2)
    corner = swap(across, "shard", 1)
    return jnp.concatenate([own, across, beside, corner], axis=0)


def blocks_by_xor(value, shard, axis):
    width = value.shape[axis] // 4
    low_bit = lax.rem(shard, 2) == 1
    high_bit = shard >= 2
    parts = [lax.slice_in_dim(value, at * width, (at + 1) * width, axis=axis) for at in range(4)]
    a, b, c, d = parts
    a, b, c, d = (
        jnp.where(low_bit, b, a), jnp.where(low_bit, a, b),
        jnp.where(low_bit, d, c), jnp.where(low_bit, c, d),
    )
    a, b, c, d = (
        jnp.where(high_bit, c, a), jnp.where(high_bit, d, b),
        jnp.where(high_bit, a, c), jnp.where(high_bit, b, d),
    )
    return jnp.concatenate([a, c, b, d], axis=axis)


def blocks_back(value, shard, axis):
    width = value.shape[axis] // 4
    a, c, b, d = [
        lax.slice_in_dim(value, at * width, (at + 1) * width, axis=axis) for at in range(4)
    ]
    low_bit = lax.rem(shard, 2) == 1
    high_bit = shard >= 2
    a, b, c, d = (
        jnp.where(high_bit, c, a), jnp.where(high_bit, d, b),
        jnp.where(high_bit, a, c), jnp.where(high_bit, b, d),
    )
    a, b, c, d = (
        jnp.where(low_bit, b, a), jnp.where(low_bit, a, b),
        jnp.where(low_bit, d, c), jnp.where(low_bit, c, d),
    )
    return jnp.concatenate([a, b, c, d], axis=axis)


def gather_rows(own):
    return lax.all_gather(own, "head", axis=0, tiled=True)


def scatter_rows(total):
    return lax.psum_scatter(total, "head", scatter_dimension=0, tiled=True).astype(F32)


def scatter_grad(grad):
    width = grad.shape[0] // 4
    near = (
        grad[: 2 * width] + swap(grad[2 * width :].astype(BF), "shard", 1).astype(F32)
    )
    own = near[:width] + swap(near[width:].astype(BF), "shard", 2).astype(F32)
    own = own.astype(BF)
    if lax.axis_size("rep") == 2:
        return own.astype(F32) + swap(own, "rep", 1).astype(F32)
    return lax.psum(own.astype(F32), "rep")


def scatter_small(blocks):
    near = blocks[:2] + swap(blocks[2:], "shard", 1)
    own = near[:1] + swap(near[1:], "shard", 2)
    if lax.axis_size("rep") == 2:
        return own + swap(own, "rep", 1)
    return lax.psum(own, "rep")


def head_sum(value):
    bit = 1
    while bit < lax.axis_size("head"):
        value = value + swap(value, "head", bit)
        bit *= 2
    return value


def forward_kernel(count, block, slopes, starts, q_ref, k_ref, v_ref, o_ref, lse_ref):
    pair = pl.program_id(0)
    key_at = lax.broadcasted_iota(jnp.int32, (block, block), 0)
    query_at = lax.broadcasted_iota(jnp.int32, (block, block), 1)
    gap = (query_at - key_at).astype(F32)
    seen = query_at >= key_at
    rows = [pl.ds(pl.multiple_of(starts[at], block), block) for at in range(count)]
    for head in range(2):
        lanes = pl.ds(head * HD, HD)
        slope = slopes[pair * 2 + head]
        tilt = gap * slope
        for at in range(count):
            query = q_ref[rows[at], lanes]
            tiles = []
            for to in range(at + 1):
                tile = contract(k_ref[rows[to], lanes], query, 1, 1)
                tile = tile - (tilt + slope * float((at - to) * block))
                if to == at:
                    tile = jnp.where(seen, tile, -1e30)
                tiles.append(tile)
            top = jnp.max(tiles[0], axis=0, keepdims=True)
            for tile in tiles[1:]:
                top = jnp.maximum(top, jnp.max(tile, axis=0, keepdims=True))
            tiles = [jnp.exp(tile - top) for tile in tiles]
            total = jnp.sum(tiles[0], axis=0, keepdims=True)
            for tile in tiles[1:]:
                total = total + jnp.sum(tile, axis=0, keepdims=True)
            share = 1.0 / total
            mixed = None
            for to in range(at + 1):
                piece = contract(v_ref[rows[to], lanes], (tiles[to] * share).astype(BF), 0, 0)
                mixed = piece if mixed is None else mixed + piece
            o_ref[rows[at], lanes] = mixed.T.astype(BF)
            lse_ref[0, pl.ds(head * count + at, 1), :] = top + jnp.log(total)


def backward_kernel(
    count, block, slopes, starts, q_ref, k_ref, v_ref, g_ref, lse_ref,
    dq_ref, dk_ref, dv_ref, dk_sum, dv_sum,
):
    pair = pl.program_id(0)
    key_at = lax.broadcasted_iota(jnp.int32, (block, block), 0)
    query_at = lax.broadcasted_iota(jnp.int32, (block, block), 1)
    gap = (query_at - key_at).astype(F32)
    seen = query_at >= key_at
    rows = [pl.ds(pl.multiple_of(starts[at], block), block) for at in range(count)]
    for head in range(2):
        lanes = pl.ds(head * HD, HD)
        slope = slopes[pair * 2 + head]
        tilt = gap * slope
        for at in reversed(range(count)):
            query = q_ref[rows[at], lanes]
            grad = g_ref[rows[at], lanes]
            lse = lse_ref[0, pl.ds(head * count + at, 1), :]
            probs, grads = [], []
            inner = None
            for to in range(at + 1):
                tile = contract(k_ref[rows[to], lanes], query, 1, 1)
                tile = tile - (tilt + (slope * float((at - to) * block) + lse))
                if to == at:
                    tile = jnp.where(seen, tile, -1e30)
                prob = jnp.exp(tile)
                prob_grad = contract(v_ref[rows[to], lanes], grad, 1, 1)
                part = jnp.sum(prob * prob_grad, axis=0, keepdims=True)
                inner = part if inner is None else inner + part
                probs.append(prob)
                grads.append(prob_grad)
            query_grad = None
            for to in range(at + 1):
                score_grad = (probs[to] * (grads[to] - inner)).astype(BF)
                piece = contract(k_ref[rows[to], lanes], score_grad, 0, 0)
                query_grad = piece if query_grad is None else query_grad + piece
                key_piece = contract(score_grad, query, 1, 0)
                value_piece = contract(probs[to].astype(BF), grad, 1, 0)
                span = pl.ds(to * block, block)
                if at == count - 1:
                    dk_sum[span, :] = key_piece
                    dv_sum[span, :] = value_piece
                else:
                    dk_sum[span, :] += key_piece
                    dv_sum[span, :] += value_piece
            dq_ref[rows[at], lanes] = (query_grad.T * HD**-0.5).astype(BF)
        for to in range(count):
            span = pl.ds(to * block, block)
            dk_ref[rows[to], lanes] = dk_sum[span, :].astype(BF)
            dv_ref[rows[to], lanes] = dv_sum[span, :].astype(BF)


def attend(qkv, slopes, starts, block):
    seq, width = qkv.shape[0], qkv.shape[1] // 3
    pairs, count = width // 128, seq // block

    def at(first):
        return pl.BlockSpec((seq, 128), lambda pair: (0, first * pairs + pair))

    scalar = pl.BlockSpec(memory_space=pltpu.SMEM)
    return pl.pallas_call(
        partial(forward_kernel, count, block),
        grid=(pairs,),
        in_specs=[scalar, scalar, at(0), at(1), at(2)],
        out_specs=[at(0), pl.BlockSpec((1, 2 * count, block), lambda pair: (pair, 0, 0))],
        out_shape=[
            jax.ShapeDtypeStruct((seq, width), BF),
            jax.ShapeDtypeStruct((pairs, 2 * count, block), F32),
        ],
        compiler_params=pltpu.CompilerParams(vmem_limit_bytes=32 * 2**20),
        name="attend",
    )(slopes, starts, qkv, qkv, qkv)


def attend_back(qkv, grad, logsum, slopes, starts, block):
    seq, width = grad.shape
    pairs, count = width // 128, seq // block

    def at(first):
        return pl.BlockSpec((seq, 128), lambda pair: (0, first * pairs + pair))

    scalar = pl.BlockSpec(memory_space=pltpu.SMEM)
    shape = jax.ShapeDtypeStruct((seq, width), BF)
    return pl.pallas_call(
        partial(backward_kernel, count, block),
        grid=(pairs,),
        in_specs=[
            scalar, scalar, at(0), at(1), at(2), at(0),
            pl.BlockSpec((1, 2 * count, block), lambda pair: (pair, 0, 0)),
        ],
        out_specs=[at(0), at(0), at(0)],
        out_shape=[shape, shape, shape],
        scratch_shapes=[pltpu.VMEM((seq, HD), F32), pltpu.VMEM((seq, HD), F32)],
        compiler_params=pltpu.CompilerParams(vmem_limit_bytes=32 * 2**20),
        name="attend_back",
    )(slopes, starts, qkv, qkv, qkv, grad, logsum)


def body(
    tokens,
    ln1_gain,
    ln1_bias,
    w_query,
    w_key,
    w_value,
    b_query,
    b_value,
    w_out,
    b_out,
    ln2_gain,
    ln2_bias,
    w_up,
    b_up,
    w_down,
    b_down,
    cotangent,
):
    shard = lax.axis_index("shard")
    place = lax.axis_index("head")
    group = lax.axis_size("head")
    heads_here = b_query.shape[0]
    width = w_query.shape[1]
    ffn = w_up.shape[1]
    feats = ln1_gain.shape[0]
    block = tokens.shape[0]

    attn_w = spread_blocks(jnp.concatenate([w_query, w_key, w_value, w_out.T], axis=1))
    small = jnp.concatenate(
        [ln1_gain, ln1_bias, b_out, ln2_gain, ln2_bias, b_down]
        + [b_query.reshape(-1), b_value.reshape(-1), b_up.reshape(-1)]
    )
    small = lax.all_gather(small, "shard", axis=0)
    rows6 = small[:, : 6 * feats].reshape(4, 6, feats)
    rows6 = rows6.transpose(1, 0, 2).reshape(6, 4 * feats).astype(F32)
    gain_one, shift_one, out_b, gain_two, shift_two, down_b = blocks_by_xor(rows6, shard, 1)
    at = 6 * feats
    step = b_query.size
    query_b = small[:, at : at + step].reshape(4, heads_here, -1).transpose(1, 0, 2).reshape(-1)
    at += step
    value_b = small[:, at : at + step].reshape(4, heads_here, -1).transpose(1, 0, 2).reshape(-1)
    at += step
    up_b = small[:, at:].reshape(4, b_up.shape[0], -1).transpose(1, 0, 2).reshape(-1).astype(F32)
    qkv_b = jnp.concatenate([query_b, jnp.zeros_like(query_b), value_b]).astype(F32)

    inputs = blocks_by_xor(tokens, shard, 1).astype(F32)
    cot = blocks_by_xor(cotangent, shard, 1)
    normed_one = gather_rows(layer_norm(inputs, gain_one, shift_one).astype(BF))
    up_w = spread_blocks(w_up)
    down_w = spread_blocks(w_down.T)
    mlp_grad = gather_rows(cot)

    qkv_w = attn_w[:, : 3 * width]
    out_w = attn_w[:, 3 * width :]
    factor = jnp.concatenate([jnp.full((width,), HD**-0.5, F32), jnp.ones((2 * width,), F32)])
    qkv = ((jnp.dot(normed_one, qkv_w, preferred_element_type=F32) + qkv_b) * factor).astype(BF)
    position = place * heads_here + jnp.arange(heads_here, dtype=jnp.int32) + 1
    slopes = jnp.exp2(-8.0 * position.astype(F32) / HEADS)
    starts = jnp.arange(group, dtype=jnp.int32) * block
    mixed, logsum = attend(qkv, slopes, starts, block)
    resid = inputs + scatter_rows(contract(mixed, out_w, 1, 1).astype(BF)) + out_b
    normed_two = gather_rows(layer_norm(resid, gain_two, shift_two).astype(BF))
    hidden_pre = jnp.dot(normed_two, up_w, preferred_element_type=F32) + up_b
    hidden = jax.nn.gelu(hidden_pre, approximate=True).astype(BF)
    hidden_grad = jnp.dot(mlp_grad, down_w, preferred_element_type=F32)
    unused, gelu_back = jax.vjp(partial(jax.nn.gelu, approximate=True), hidden_pre)
    pre_grad_f = gelu_back(hidden_grad)[0]
    pre_grad = pre_grad_f.astype(BF)
    second_grad = scatter_rows(contract(pre_grad, up_w, 1, 1).astype(BF))
    output = resid + scatter_rows(contract(hidden, down_w, 1, 1).astype(BF)) + down_b
    output = blocks_back(output.astype(BF), shard, 1)
    upstream = cot.astype(F32)
    down_b_grad = jnp.sum(upstream, axis=0)
    down_w_grad = scatter_grad(contract(mlp_grad, hidden, 0, 0))
    up_w_grad = scatter_grad(contract(normed_two, pre_grad, 0, 0))
    up_b_grad = jnp.sum(pre_grad.astype(F32), axis=0)
    unused, norm_back = jax.vjp(layer_norm, resid, gain_two, shift_two)
    resid_part, gain_two_grad, shift_two_grad = norm_back(second_grad)
    resid_grad = upstream + resid_part
    out_b_grad = jnp.sum(resid_grad, axis=0)
    attn_grad = gather_rows(resid_grad.astype(BF))
    mixed_grad = jnp.dot(attn_grad, out_w, preferred_element_type=F32).astype(BF)
    out_w_grad = scatter_grad(contract(attn_grad, mixed, 0, 0))
    query_grad, key_grad, value_grad = attend_back(qkv, mixed_grad, logsum, slopes, starts, block)
    qkv_grad = jnp.concatenate([query_grad, key_grad, value_grad], axis=1)
    first_grad = scatter_rows(contract(qkv_grad, qkv_w, 1, 1).astype(BF))
    qkv_w_grad = scatter_grad(contract(normed_one, qkv_grad, 0, 0))
    query_b_grad = jnp.sum(query_grad.astype(F32), axis=0)
    value_b_grad = jnp.sum(value_grad.astype(F32), axis=0)
    unused, first_back = jax.vjp(layer_norm, inputs, gain_one, shift_one)
    input_part, gain_one_grad, shift_one_grad = first_back(first_grad)
    input_grad = blocks_back((resid_grad + input_part).astype(BF), shard, 1)

    def feature_blocks(values):
        return values.reshape(-1, 4, feats).transpose(1, 0, 2).reshape(4, -1)

    def bias_blocks(values, rows):
        parts = values.reshape(rows, 4, -1).transpose(1, 0, 2).reshape(4, -1)
        return blocks_by_xor(parts, shard, 0)

    late = scatter_small(
        jnp.concatenate(
            [
                feature_blocks(jnp.stack([gain_one_grad, shift_one_grad])),
                bias_blocks(jnp.stack([query_b_grad, value_b_grad]), 2 * heads_here),
            ],
            axis=1,
        )
    )
    late_stats = head_sum(late[:, : 2 * feats]).reshape(2, feats)
    late_bias = late[:, 2 * feats :].reshape(2, heads_here, -1)
    early = scatter_small(
        jnp.concatenate(
            [
                feature_blocks(jnp.stack([out_b_grad, gain_two_grad, shift_two_grad, down_b_grad])),
                bias_blocks(up_b_grad, b_up.shape[0]),
            ],
            axis=1,
        )
    )
    early_stats = head_sum(early[:, : 4 * feats]).reshape(4, feats)
    early_bias = early[:, 4 * feats :].reshape(b_up.shape[0], -1)

    return (
        output,
        input_grad,
        late_stats[0],
        late_stats[1],
        qkv_w_grad[:, :width],
        qkv_w_grad[:, width : 2 * width],
        qkv_w_grad[:, 2 * width :],
        late_bias[0],
        late_bias[1],
        out_w_grad.T,
        early_stats[0],
        early_stats[1],
        early_stats[2],
        up_w_grad,
        early_bias,
        down_w_grad.T,
        early_stats[3],
    )


def solution(mesh):
    return jax.shard_map(
        body,
        mesh=mesh,
        in_specs=(
            P(("rep", "shard", "head"), None),
            P("shard"),
            P("shard"),
            P("shard", "head"),
            P("shard", "head"),
            P("shard", "head"),
            P("head", "shard"),
            P("head", "shard"),
            P("head", "shard"),
            P("shard"),
            P("shard"),
            P("shard"),
            P("shard", "head"),
            P("head", "shard"),
            P("head", "shard"),
            P("shard"),
            P(("rep", "shard", "head"), None),
        ),
        out_specs=(
            P(("rep", "shard", "head"), None),
            P(("rep", "shard", "head"), None),
            P("shard"),
            P("shard"),
            P("shard", "head"),
            P("shard", "head"),
            P("shard", "head"),
            P("head", "shard"),
            P("head", "shard"),
            P("head", "shard"),
            P("shard"),
            P("shard"),
            P("shard"),
            P("shard", "head"),
            P("head", "shard"),
            P("head", "shard"),
            P("shard"),
        ),
        check_vma=False,
    )
```
